32 devices in a mesh: seq: 8 (over y, x, core), wsh: 4 (over z).
Axes of the slice: x: 2, y: 2, z: 4, core: 2. Of those that a mesh axis runs over, the one named last changes fastest.
Arguments:
- tokens: bfloat16 [4, 8192, 768], P('wsh', 'seq'), may hold values from -6 to 6
- positions: int32 [4, 8192], P('wsh', 'seq'), may hold values from 0 to 8191, as said below
- w_qkv: bfloat16 [768, 2304], P('wsh'), may hold values from -0.21875 to 0.21875
- w_attn: bfloat16 [768, 768], P('wsh'), may hold values from -1.5 to 1.5
- w_in: bfloat16 [768, 2304], P('wsh'), may hold values from -0.21875 to 0.21875
- w_down: bfloat16 [1152, 768], P('wsh'), may hold values from -0.375 to 0.375
- gain_attn: bfloat16 [768], P('wsh'), may hold values from 0.5 to 1.5
- gain_mlp: bfloat16 [768], P('wsh'), may hold values from 0.5 to 1.5
- grad_out: bfloat16 [4, 8192, 768], P('wsh', 'seq'), may hold values from -6 to 6
Outputs:
- mixed: bfloat16 [4, 8192, 768], P('wsh', 'seq')
- grad_tokens: float32 [4, 8192, 768], P('wsh', 'seq')
- grad_qkv: float32 [768, 2304], P('wsh')
- grad_attn: float32 [768, 768], P('wsh')
- grad_in: float32 [768, 2304], P('wsh')
- grad_down: float32 [1152, 768], P('wsh')
- grad_gain_attn: float32 [768], P('wsh')
- grad_gain_mlp: float32 [768], P('wsh')
The draws below stay inside these ranges and needn't reach their ends.
Inputs may be any that keep to these rules, and one draw needn't show every extreme that they name: In each stream the positions go up by one from token to token inside a sequence and restart at 0 where a new sequence begins. Each stream holds three sequences; the first ends at position 8191, the middle one reaches from the first device of seq to the last.
All inputs are finite; a program needn't handle non-finite values.
Results may differ from the reference program's by a relative error of at most 0.02.
Values may be sent and summed in bfloat16 or wider, within the bound.
A program may use at most 192 MiB of HBM per device.

```python
import jax
import jax.numpy as jnp
from jax import lax

D = 768
HEADS = 12
HEAD_DIM = 64
FF = 1152
HALF = 64
QBLK = 512
TOK_DEV = 1024
GROUPS = 4
GROUP_TOK = 8192


def draw_positions(key, part):
    key = jax.random.fold_in(key, 11)
    head_key, tail_key = jax.random.split(key, 2)
    head_len = jax.random.randint(head_key, (GROUPS, 1), 1, TOK_DEV // 2 + 1)
    tail_len = jax.random.randint(tail_key, (GROUPS, 1), 1, TOK_DEV // 2 + 1)
    leading = GROUP_TOK - head_len
    indices = jnp.arange(GROUP_TOK, dtype=jnp.int32)[None, :]
    finish = GROUP_TOK - tail_len
    placed = jnp.where(indices < head_len, indices + leading, jnp.where(indices < finish, indices - head_len, indices - finish))
    return placed.astype(jnp.int32)


def level_of(rng, extent, cuts, least, top_value):
    def one(dim, shards_of):
        steps = jax.random.uniform(jax.random.fold_in(jax.random.fold_in(rng, 6), dim), (shards_of,), jnp.float32, least / len(cuts), top_value / len(cuts))
        return jnp.repeat(jnp.exp(steps), extent[dim] // shards_of).reshape((-1,) + (1,) * (len(extent) - dim - 1))

    gain = one(*cuts[0])
    for cut in cuts[1:]:
        gain = gain * one(*cut)
    return gain


def noise(own_key, dims, scale, reach, pieces=(), held_as=jnp.bfloat16):
    result = jax.random.normal(own_key, dims, jnp.float32) * scale
    if len(pieces) > 0:
        result = level_of(own_key, dims, pieces, -0.22, 0.18) * result
    return jnp.clip(result, min=-reach, max=reach).astype(held_as)


def setup_inputs(seed: int = 0) -> dict:
    key_list = jax.random.split(jax.random.key(seed), 10)
    return {
        "tokens": noise(key_list[0], (GROUPS, GROUP_TOK, D), 1.0, 6.0, ((0, 4), (1, 8))),
        "positions": draw_positions(jax.random.fold_in(key_list[9], 71), 0),
        "w_qkv": noise(key_list[2], (D, 3 * D), D ** -0.5, 0.21875, ((0, 4),)),
        "w_attn": noise(key_list[3], (D, D), (D // 48) ** -0.5, 1.5, ((0, 4),)),
        "w_in": noise(key_list[4], (D, 2 * FF), D ** -0.5, 0.21875, ((0, 4),)),
        "w_down": noise(key_list[5], (FF, D), (FF // 4) ** -0.5, 0.375, ((0, 4),)),
        "gain_attn": jnp.clip(1.0 + 0.1 * jax.random.normal(key_list[6], (D,), jnp.float32), 0.5, 1.5).astype(jnp.bfloat16),
        "gain_mlp": jnp.clip(1.0 + 0.1 * jax.random.normal(key_list[7], (D,), jnp.float32), 0.5, 1.5).astype(jnp.bfloat16),
        "grad_out": noise(key_list[8], (GROUPS, GROUP_TOK, D), 1.0, 6.0, ((0, 4), (1, 8))),
    }


EPS = 1e-05
NEGATIVE = -1e+30
PRECISE = lax.Precision.HIGHEST

@jax.custom_vjp
def low(v):
    return lax.optimization_barrier(v.astype(jnp.bfloat16)).astype(jnp.float32)

@jax.custom_vjp
def low_back(v):
    return v

def low_keep(v):
    return (low(v), None)

def low_pass(kept, grad):
    return (grad,)

def back_keep(v):
    return (v, None)

def back_low(kept, grad):
    return (low(grad),)
low.defvjp(low_keep, low_pass)
low_back.defvjp(back_keep, back_low)

def layer_norm(values, scales):
    centre = lax.optimization_barrier(jnp.mean(values, axis=-1, keepdims=True))
    shifted = values - centre
    spread = lax.optimization_barrier(jnp.mean(shifted * shifted, axis=-1, keepdims=True))
    return shifted * lax.rsqrt(spread + EPS) * scales

def rotary(values, places):
    halves = values.shape[-1] // 2
    exponent = jnp.arange(halves, dtype=jnp.float32) * (2.0 / values.shape[-1])
    frequency = jnp.power(jnp.float32(10000.0), -exponent)
    angles = places.astype(jnp.float32)[:, None] * frequency[None, :]
    cosine = jnp.cos(angles)[:, None, :]
    sine = jnp.sin(angles)[:, None, :]
    first = values[..., :halves]
    second = values[..., halves:]
    return jnp.concatenate([first * cosine - second * sine, second * cosine + first * sine], axis=-1)

def banded(row_ids, col_ids, row_places, col_places, limit):
    near = jnp.abs(row_ids[:, None] - col_ids[None, :]) <= HALF
    inside = ((col_ids >= 0) & (col_ids < limit))[None, :]
    same = col_places[None, :] - row_places[:, None] == col_ids[None, :] - row_ids[:, None]
    return near & inside & same

def product(left, right):
    return jnp.dot(left, right, precision=PRECISE)

def attend(queries, keys_in, values_in, places):
    span = QBLK + 2 * HALF
    padded_keys = jnp.pad(keys_in, ((HALF, HALF), (0, 0), (0, 0)))
    padded_values = jnp.pad(values_in, ((HALF, HALF), (0, 0), (0, 0)))
    padded_places = jnp.pad(places, (HALF, HALF))

    def one_block(block_index):
        offset = (block_index * QBLK).astype(jnp.int32)
        query_block = lax.dynamic_slice_in_dim(queries, offset, QBLK, 0)
        key_block = lax.dynamic_slice_in_dim(padded_keys, offset, span, 0)
        value_block = lax.dynamic_slice_in_dim(padded_values, offset, span, 0)
        row_places = lax.dynamic_slice_in_dim(places, offset, QBLK, 0)
        col_places = lax.dynamic_slice_in_dim(padded_places, offset, span, 0)
        row_ids = offset + jnp.arange(QBLK, dtype=jnp.int32)
        col_ids = offset - HALF + jnp.arange(span, dtype=jnp.int32)
        allowed = banded(row_ids, col_ids, row_places, col_places, GROUP_TOK)
        scores = low_back(jnp.einsum('qhd,khd->hqk', query_block, key_block, precision=PRECISE) * HEAD_DIM ** (-0.5))
        masked = jnp.where(allowed[None], scores, NEGATIVE)
        peak = lax.optimization_barrier(jnp.max(masked, axis=-1, keepdims=True))
        raised = jnp.exp(masked - peak)
        probs = raised / lax.optimization_barrier(jnp.sum(raised, axis=-1, keepdims=True))
        return jnp.einsum('hqk,khd->qhd', low(probs), value_block, precision=PRECISE)
    block_outs = lax.map(jax.checkpoint(one_block), jnp.arange(GROUP_TOK // QBLK, dtype=jnp.int32))
    return block_outs.reshape(GROUP_TOK, HEADS * HEAD_DIM)

def forward(x_in, places, w_qkv, w_attn, w_in, w_down, gain_attn, gain_mlp):
    model_width = HEADS * HEAD_DIM
    normed_attn = low(layer_norm(x_in, gain_attn))
    qkv = low_back(product(normed_attn, w_qkv))
    queries = qkv[:, :model_width].reshape(-1, HEADS, HEAD_DIM)
    keys_all = qkv[:, model_width:2 * model_width].reshape(-1, HEADS, HEAD_DIM)
    values_all = qkv[:, 2 * model_width:].reshape(-1, HEADS, HEAD_DIM)
    rot_q = low(rotary(queries, places))
    rot_k = low(rotary(keys_all, places))
    vals = low(values_all)
    context = low(low_back(attend(rot_q, rot_k, vals, places)))
    resid = x_in + low_back(product(context, w_attn))
    normed_mlp = low(layer_norm(resid, gain_mlp))
    gate_up = low_back(product(normed_mlp, w_in))
    hidden = low(jax.nn.gelu(gate_up[:, :FF], approximate=False) * gate_up[:, FF:])
    return resid + low_back(product(hidden, w_down))

def reference(tokens, positions, w_qkv, w_attn, w_in, w_down, gain_attn, gain_mlp, grad_out):
    weights = (w_qkv.astype(jnp.float32), w_attn.astype(jnp.float32), w_in.astype(jnp.float32), w_down.astype(jnp.float32), gain_attn.astype(jnp.float32), gain_mlp.astype(jnp.float32))

    def one_group(carry, items):
        stream, places, cotangent = items

        def apply(x_in, *params):
            return forward(x_in, places, *params)
        output, pull = jax.vjp(apply, stream.astype(jnp.float32), *weights)
        grads = pull(cotangent.astype(jnp.float32))
        summed = tuple((acc + part for acc, part in zip(carry, grads[1:])))
        return (summed, (output.astype(jnp.bfloat16), grads[0]))
    initial = tuple((jnp.zeros(w.shape, jnp.float32) for w in weights))
    sums, (mixed, grad_tokens) = lax.scan(one_group, initial, (tokens, positions, grad_out))
    return (mixed, grad_tokens, sums[0], sums[1], sums[2], sums[3], sums[4], sums[5])
```

```python
import functools

import jax
import jax.numpy as jnp
from jax import lax
from jax.experimental import pallas as pl
from jax.experimental.pallas import tpu as pltpu
from jax.sharding import PartitionSpec as P

HEADS = 12
HALF = 64
HEAD_DIM = 64
PAIR = 2 * HEAD_DIM
EPS = 1e-05
NEGATIVE = -1e30
QROWS = 128
ROWS = 256
SPLIT = 8
VMEM_LIMIT = 56 * 1024 * 1024
F32 = jnp.float32
BF16 = jnp.bfloat16
LAST = (((1,), (1,)), ((), ()))
FIRST = (((0,), (0,)), ((), ()))


def flip(count, bit):
    return [(i, i ^ bit) for i in range(count)]


def orders():
    count = lax.axis_size("seq")
    low = []
    bit = 1
    while bit < min(count, SPLIT):
        low.append(bit)
        bit *= 2
    high = []
    while bit < count:
        high.append(bit)
        bit *= 2
    return low, low[:1] + low[1:][::-1], high


def gather_line(own):
    count = lax.axis_size("wsh")
    here = lax.axis_index("wsh")
    upward = [(i, i + 1) for i in range(count - 1)]
    downward = [(j, i) for i, j in upward]
    ups, downs = [own], [own]
    for _ in range(count - 1):
        ups.append(lax.ppermute(ups[-1], "wsh", upward))
        downs.append(lax.ppermute(downs[-1], "wsh", downward))
    stacked = jnp.stack(ups[:0:-1] + [own] + downs[1:])
    return lax.dynamic_slice_in_dim(stacked, count - 1 - here, count, 0)


def gather_seq(block, order):
    here = lax.axis_index("seq")
    count = lax.axis_size("seq")
    for bit in order[::-1]:
        other = lax.ppermute(block, "seq", flip(count, bit))
        upper = (here & bit) > 0
        block = jnp.concatenate(
            [jnp.where(upper, other, block), jnp.where(upper, block, other)], axis=1
        )
    return block


def own_piece(pieces, order):
    here = lax.axis_index("seq")
    place = jnp.int32(0)
    for bit in order:
        place = place * 2 + jnp.where((here & bit) > 0, 1, 0)
    return lax.dynamic_slice_in_dim(pieces, place, 1, 0)


def gather_weight(pieces):
    first, second, _ = orders()
    half = pieces.shape[2] // 2
    outs = []
    own = [own_piece(pieces[:, :, :half], first), own_piece(pieces[:, :, half:], second)]
    lined = gather_line(jnp.concatenate(own, axis=2))
    outs.append(gather_seq(lined[:, 0][:, None, :, :half], first))
    outs.append(gather_seq(lined[:, 0][:, None, :, half:], second))
    return jnp.concatenate(outs, axis=3)


def reduce_half(block, order, high):
    here = lax.axis_index("seq")
    count = lax.axis_size("seq")
    for bit in order:
        size = block.shape[1] // 2
        upper = (here & bit) > 0
        send = jnp.where(upper, block[:, :size], block[:, size:])
        keep = jnp.where(upper, block[:, size:], block[:, :size])
        block = keep + lax.ppermute(send, "seq", flip(count, bit))
    for bit in high:
        block = block + lax.ppermute(block, "seq", flip(count, bit))
    lines = lax.axis_size("wsh")
    row = lax.axis_index("wsh")
    from_below = from_above = None
    for step in range(lines - 1):
        up = lax.dynamic_slice_in_dim(block, jnp.clip(lines - 1 - step + row, 0, lines - 1), 1, 0)
        down = lax.dynamic_slice_in_dim(block, jnp.clip(step - (lines - 1 - row), 0, lines - 1), 1, 0)
        if step > 0:
            up = up + from_below
            down = down + from_above
        from_below = lax.ppermute(up, "wsh", [(i, i + 1) for i in range(step + 1)])
        from_above = lax.ppermute(
            down, "wsh", [(lines - 1 - i, lines - 2 - i) for i in range(step + 1)]
        )
    own = lax.dynamic_slice_in_dim(block, row, 1, 0)
    total = own + from_below + from_above
    return gather_seq(total, order)[0]


def reduce_grad(block):
    first, second, high = orders()
    half = block.shape[3] // 2
    return jnp.concatenate(
        [
            reduce_half(block[..., :half], first, high),
            reduce_half(block[..., half:], second, high),
        ],
        axis=2,
    )


def fold(block):
    size = block.shape[-2] // 3
    return jnp.concatenate([block[..., i * size : (i + 1) * size, :] for i in range(3)], axis=-1)


def unfold(block):
    width = block.shape[-1] // 3
    return jnp.concatenate([block[..., i * width : (i + 1) * width] for i in range(3)], axis=-2)


def pack(lead, w_in, w_attn, w_down):
    def cut(array):
        return array.reshape(lead + (-1, array.shape[-1]))

    return jnp.concatenate([cut(w_in), fold(cut(w_attn)), fold(cut(w_down))], axis=-2)


def unpack(block, rows_in, rows_attn):
    one = block[..., :rows_in, :]
    two = unfold(block[..., rows_in : rows_in + rows_attn // 3, :])
    three = unfold(block[..., rows_in + rows_attn // 3 :, :])
    return tuple(part.reshape(-1, part.shape[-1]) for part in (one, two, three))


def sum_small(vector):
    for axis in ("seq", "wsh"):
        count = lax.axis_size(axis)
        bit = 1
        while bit < count:
            vector = vector + lax.ppermute(vector, axis, flip(count, bit))
            bit *= 2
    return vector


def neighbours(low_edge, high_edge):
    count = lax.axis_size("seq")
    forward = [(i, i + 1) for i in range(count - 1)]
    backward = [(j, i) for i, j in forward]
    return lax.ppermute(high_edge, "seq", forward), lax.ppermute(low_edge, "seq", backward)


def swap(values):
    lane = lax.broadcasted_iota(jnp.int32, values.shape, 1)
    quarter = HEAD_DIM // 2
    return jnp.where(
        lane % HEAD_DIM < quarter,
        pltpu.roll(values, PAIR - quarter, 1),
        pltpu.roll(values, quarter, 1),
    )


def normalise(values):
    centre = jnp.mean(values, axis=-1, keepdims=True)
    shifted = values - centre
    factor = lax.rsqrt(jnp.mean(shifted * shifted, axis=-1, keepdims=True) + EPS)
    return shifted * factor, factor


def project_kernel(x_ref, gain_ref, w_ref, cos_ref, sin_ref, normed_ref, q_ref, kv_ref):
    width = x_ref.shape[1]
    normed, _ = normalise(x_ref[...].astype(F32))
    low = (normed * gain_ref[...].astype(F32)).astype(BF16)
    normed_ref[...] = low
    cosine, sine = cos_ref[...], sin_ref[...]
    scale = HEAD_DIM ** (-0.5)
    for part in range(2):
        raw = jnp.dot(
            low, w_ref[:, part * width : (part + 1) * width], preferred_element_type=F32
        )
        for start in range(0, width, PAIR):
            piece = raw[:, start : start + PAIR]
            turned = (piece * cosine + swap(piece) * sine).astype(BF16)
            if part == 0:
                q_ref[:, start : start + PAIR] = turned * jnp.asarray(scale, BF16)
            else:
                kv_ref[:, start : start + PAIR] = turned
    kv_ref[:, width:] = jnp.dot(
        low, w_ref[:, 2 * width :], preferred_element_type=F32
    ).astype(BF16)


def both(pair):
    lane = lax.broadcasted_iota(jnp.int32, pair.shape, 1)
    zero = jnp.zeros_like(pair)
    left = jnp.where(lane < HEAD_DIM, pair, zero)
    right = jnp.where(lane < HEAD_DIM, zero, pair)
    return jnp.concatenate([left, right], axis=0)


def merge(stacked):
    rows = stacked.shape[0] // 2
    lane = lax.broadcasted_iota(jnp.int32, (rows, stacked.shape[1]), 1)
    return jnp.where(lane < HEAD_DIM, stacked[:rows], stacked[rows:])


def attend_kernel(q_ref, kv_ref, row_ref, col_ref, context_ref, probs_ref):
    width = q_ref.shape[1]
    span = QROWS + 2 * HALF
    offset = pl.multiple_of(pl.program_id(0) * QROWS, QROWS)
    row = lax.broadcasted_iota(jnp.int32, (QROWS, span), 0)
    col = lax.broadcasted_iota(jnp.int32, (QROWS, span), 1)
    near = (col >= row) & (col <= row + 2 * HALF)
    allowed = near & (row_ref[...] == col_ref[0])
    bias = jnp.where(allowed, 0.0, NEGATIVE)
    bias = jnp.concatenate([bias, bias], axis=0)
    for pair in range(width // PAIR):
        lanes = slice(pair * PAIR, (pair + 1) * PAIR)
        queries = both(q_ref[:, lanes])
        keys = kv_ref[pl.ds(offset, span), lanes]
        values = kv_ref[pl.ds(offset, span), slice(width + pair * PAIR, width + (pair + 1) * PAIR)]
        scores = lax.dot_general(queries, keys, LAST, preferred_element_type=F32)
        scores = jnp.where(bias < 0.0, NEGATIVE, scores)
        raised = jnp.exp(scores - jnp.max(scores, axis=-1, keepdims=True))
        probs = raised * (1.0 / jnp.sum(raised, axis=-1, keepdims=True))
        low = probs.astype(BF16)
        probs_ref[0, pair] = low
        context = jnp.dot(low, values, preferred_element_type=F32)
        context_ref[:, lanes] = merge(context).astype(BF16)


def mlp_kernel(
    x_ref, context_ref, dy_ref, gain_ref, w_attn_ref, w_in_ref, w_down_ref,
    mixed_ref, normed_ref, hidden_ref, d_gate_ref, d_resid_ref, d_low_ref, d_context_ref, d_gain_ref,
):
    hidden_width = w_down_ref.shape[0]
    scales = gain_ref[...].astype(F32)
    resid = x_ref[...].astype(F32) + jnp.dot(
        context_ref[...], w_attn_ref[...], preferred_element_type=F32
    )
    normed, factor = normalise(resid)
    low = (normed * scales).astype(BF16)
    normed_ref[...] = low
    dy = dy_ref[...]
    mixed = resid
    d_normed = jnp.zeros_like(resid)
    step = hidden_width // 3
    for start in range(0, hidden_width, step):
        here = slice(start, start + step)
        there = slice(hidden_width + start, hidden_width + start + step)
        gate = jnp.dot(low, w_in_ref[:, here], preferred_element_type=F32)
        up = jnp.dot(low, w_in_ref[:, there], preferred_element_type=F32)
        d_hidden = lax.dot_general(dy, w_down_ref[here, :], LAST, preferred_element_type=F32)
        cdf = 0.5 + 0.5 * lax.erf(gate * (0.5**0.5))
        pdf = jnp.exp(-0.5 * gate * gate) * 0.3989422804014327
        gelu = gate * cdf
        hidden = (gelu * up).astype(BF16)
        hidden_ref[:, here] = hidden
        mixed = mixed + jnp.dot(hidden, w_down_ref[here, :], preferred_element_type=F32)
        d_gate = (d_hidden * up * (cdf + gate * pdf)).astype(BF16)
        d_up = (d_hidden * gelu).astype(BF16)
        d_gate_ref[:, here] = d_gate
        d_gate_ref[:, there] = d_up
        d_normed = d_normed + lax.dot_general(
            d_gate, w_in_ref[:, here], LAST, preferred_element_type=F32
        )
        d_normed = d_normed + lax.dot_general(
            d_up, w_in_ref[:, there], LAST, preferred_element_type=F32
        )
    mixed_ref[...] = mixed.astype(BF16)
    partial = jnp.sum(d_normed * normed, axis=0, keepdims=True)

    @pl.when(pl.program_id(0) == 0)
    def _():
        d_gain_ref[...] = jnp.zeros_like(d_gain_ref)

    d_gain_ref[...] += partial
    scaled = d_normed * scales
    mean = jnp.mean(scaled, axis=-1, keepdims=True)
    cross = jnp.mean(scaled * normed, axis=-1, keepdims=True)
    d_resid = dy.astype(F32) + factor * (scaled - mean - normed * cross)
    d_resid_ref[...] = d_resid
    d_low = d_resid.astype(BF16)
    d_low_ref[...] = d_low
    d_context_ref[...] = lax.dot_general(
        d_low, w_attn_ref[...], LAST, preferred_element_type=F32
    ).astype(BF16)


def attend_back_kernel(
    q_ref, kv_ref, probs_ref, d_ref, cos_ref, sin_ref, d_q_ref, d_kv_ref
):
    width = q_ref.shape[1]
    span = QROWS + 2 * HALF
    offset = pl.multiple_of(pl.program_id(0) * QROWS, QROWS)

    @pl.when(pl.program_id(0) == 0)
    def _():
        d_kv_ref[...] = jnp.zeros_like(d_kv_ref)

    cosine, sine = cos_ref[...], sin_ref[...]
    scale = HEAD_DIM ** (-0.5)
    for pair in range(width // PAIR):
        lanes = slice(pair * PAIR, (pair + 1) * PAIR)
        value_lanes = slice(width + pair * PAIR, width + (pair + 1) * PAIR)
        queries = both(q_ref[:, lanes])
        d_out = both(d_ref[:, lanes])
        keys = kv_ref[pl.ds(offset, span), lanes]
        values = kv_ref[pl.ds(offset, span), value_lanes]
        low = probs_ref[0, pair]
        probs = low.astype(F32)
        d_probs = lax.dot_general(d_out, values, LAST, preferred_element_type=F32)
        delta = jnp.sum(d_probs * probs, axis=-1, keepdims=True)
        d_scores = (probs * (d_probs - delta)).astype(BF16)
        d_kv_ref[pl.ds(offset, span), value_lanes] += lax.dot_general(
            low, d_out, FIRST, preferred_element_type=F32
        )
        d_kv_ref[pl.ds(offset, span), lanes] += lax.dot_general(
            d_scores, queries, FIRST, preferred_element_type=F32
        )
        d_q = merge(jnp.dot(d_scores, keys, preferred_element_type=F32)) * scale
        d_q_ref[:, lanes] = (d_q * cosine - swap(d_q) * sine).astype(BF16)


def finish_kernel(d_q_ref, d_kv_ref, low_ref, high_ref, cos_ref, sin_ref, d_qkv_ref):
    width = d_q_ref.shape[1]
    step = pl.program_id(0)
    offset = pl.multiple_of(step * ROWS, ROWS)
    first = step == 0
    last = step == pl.num_programs(0) - 1
    cosine, sine = cos_ref[...], sin_ref[...]
    d_qkv_ref[:, :width] = d_q_ref[...]
    for start in range(0, 2 * width, PAIR):
        lanes = slice(start, start + PAIR)
        block = d_kv_ref[pl.ds(offset + HALF, ROWS), lanes]
        low = jnp.where(first, low_ref[:, lanes].astype(F32), 0.0)
        high = jnp.where(last, high_ref[:, lanes].astype(F32), 0.0)
        block = jnp.concatenate(
            [block[:HALF] + low, block[HALF : ROWS - HALF], block[ROWS - HALF :] + high], axis=0
        )
        if start < width:
            block = block * cosine - swap(block) * sine
        d_qkv_ref[:, width + start : width + start + PAIR] = block.astype(BF16)


def norm_back_kernel(x_ref, gain_ref, d_qkv_ref, w_ref, d_resid_ref, d_tokens_ref, d_gain_ref):
    normed, factor = normalise(x_ref[...].astype(F32))
    d_normed = lax.dot_general(d_qkv_ref[...], w_ref[...], LAST, preferred_element_type=F32)
    partial = jnp.sum(d_normed * normed, axis=0, keepdims=True)

    @pl.when(pl.program_id(0) == 0)
    def _():
        d_gain_ref[...] = jnp.zeros_like(d_gain_ref)

    d_gain_ref[...] += partial
    scaled = d_normed * gain_ref[...].astype(F32)
    mean = jnp.mean(scaled, axis=-1, keepdims=True)
    cross = jnp.mean(scaled * normed, axis=-1, keepdims=True)
    d_tokens_ref[...] = d_resid_ref[...] + factor * (scaled - mean - normed * cross)


def by_rows(rows, width):
    return pl.BlockSpec((rows, width), lambda i: (i, 0))


def whole(shape):
    return pl.BlockSpec(shape, lambda i: (0,) * len(shape))


def call(kernel, steps, inputs, specs, outs, out_specs, flops):
    size = sum(a.size * a.dtype.itemsize for a in inputs)
    size += sum(o.size * o.dtype.itemsize for o in outs)
    return pl.pallas_call(
        kernel,
        grid=(steps,),
        in_specs=specs,
        out_specs=out_specs,
        out_shape=outs,
        compiler_params=pltpu.CompilerParams(
            dimension_semantics=("arbitrary",), vmem_limit_bytes=VMEM_LIMIT
        ),
        cost_estimate=pl.CostEstimate(flops=flops, bytes_accessed=size, transcendentals=0),
    )(*inputs)


def shape(dims, dtype):
    return jax.ShapeDtypeStruct(dims, dtype)


def body(tokens, positions, w_qkv, w_attn, w_in, w_down, gain_attn, gain_mlp, grad_out):
    rows, width = tokens.shape[1:]
    lines = lax.axis_size("wsh")
    hidden = w_down.shape[0] * lines
    x = tokens[0]
    dy = grad_out[0]
    places = positions[0]
    seq = lax.axis_index("seq")
    seqs = lax.axis_size("seq")

    split = min(SPLIT, seqs)
    gains = gather_line(jnp.stack([gain_attn, gain_mlp]))
    gain_a = gains[:, 0].reshape(1, width)
    gain_m = gains[:, 1].reshape(1, width)
    full_qkv = gather_weight(w_qkv.reshape(split, -1, 3 * width)).reshape(width, 3 * width)
    packed = gather_weight(pack((split,), w_in, w_attn, w_down))
    rows_in = w_in.shape[0] // split
    rows_attn = w_attn.shape[0] // split
    full_in, full_attn, full_down = unpack(packed, rows_in, rows_attn)

    base = seq * rows
    ids = places - (base + jnp.arange(rows, dtype=jnp.int32))
    below, above = neighbours(ids[:HALF], ids[rows - HALF :])
    nowhere = jnp.int32(-(1 << 30))
    below = jnp.where(seq == 0, nowhere, below)
    above = jnp.where(seq == seqs - 1, nowhere, above)
    ids_wide = jnp.concatenate([below, ids, above])
    blocks = rows // QROWS
    span = QROWS + 2 * HALF
    cols = jnp.stack([ids_wide[i * QROWS : i * QROWS + span] for i in range(blocks)])[:, None, :]

    lane = jnp.arange(PAIR, dtype=jnp.int32)
    quarter = HEAD_DIM // 2
    exponent = (lane % quarter).astype(F32) * (2.0 / HEAD_DIM)
    frequency = jnp.power(F32(10000.0), -exponent)
    angles = places.astype(F32)[:, None] * frequency[None, :]
    cosine = jnp.cos(angles)
    sine = jnp.where(lane % HEAD_DIM < quarter, -1.0, 1.0)[None, :] * jnp.sin(angles)

    big = rows // ROWS
    normed_attn, queries, kv = call(
        project_kernel, big, (x, gain_a, full_qkv, cosine, sine),
        [by_rows(ROWS, width), whole((1, width)), whole((width, 3 * width)),
         by_rows(ROWS, PAIR), by_rows(ROWS, PAIR)],
        [shape((rows, width), BF16), shape((rows, width), BF16), shape((rows, 2 * width), BF16)],
        [by_rows(ROWS, width), by_rows(ROWS, width), by_rows(ROWS, 2 * width)],
        6 * rows * width * width,
    )
    kv_below, kv_above = neighbours(kv[:HALF], kv[rows - HALF :])
    kv_wide = jnp.concatenate([kv_below, kv, kv_above], axis=0)
    pairs = width // PAIR
    probs_spec = pl.BlockSpec((1, pairs, 2 * QROWS, span), lambda i: (i, 0, 0, 0))
    attend_flops = 4 * blocks * pairs * 2 * QROWS * span * PAIR
    context, probs = call(
        attend_kernel, blocks, (queries, kv_wide, ids[:, None], cols),
        [by_rows(QROWS, width), whole((rows + 2 * HALF, 2 * width)), by_rows(QROWS, 1),
         pl.BlockSpec((1, 1, span), lambda i: (i, 0, 0))],
        [shape((rows, width), BF16), shape((blocks, pairs, 2 * QROWS, span), BF16)],
        [by_rows(QROWS, width), probs_spec],
        attend_flops,
    )
    mixed, normed_mlp, hidden_low, d_gate, d_resid, d_low, d_context, d_gain_m = call(
        mlp_kernel, big, (x, context, dy, gain_m, full_attn, full_in, full_down),
        [by_rows(ROWS, width), by_rows(ROWS, width), by_rows(ROWS, width), whole((1, width)),
         whole((width, width)), whole((width, 2 * hidden)), whole((hidden, width))],
        [shape((rows, width), BF16), shape((rows, width), BF16), shape((rows, hidden), BF16),
         shape((rows, 2 * hidden), BF16), shape((rows, width), F32), shape((rows, width), BF16),
         shape((rows, width), BF16), shape((1, width), F32)],
        [by_rows(ROWS, width), by_rows(ROWS, width), by_rows(ROWS, hidden),
         by_rows(ROWS, 2 * hidden), by_rows(ROWS, width), by_rows(ROWS, width),
         by_rows(ROWS, width), whole((1, width))],
        2 * rows * width * (2 * width + 6 * hidden),
    )

    def weight_grad(left, right):
        return lax.dot_general(left, right, FIRST, preferred_element_type=F32).astype(BF16)

    grads_packed = pack(
        (lines, split),
        weight_grad(normed_mlp, d_gate),
        weight_grad(context, d_low),
        weight_grad(hidden_low, dy),
    )
    out_packed = reduce_grad(grads_packed)

    d_q, d_kv = call(
        attend_back_kernel, blocks, (queries, kv_wide, probs, d_context, cosine, sine),
        [by_rows(QROWS, width), whole((rows + 2 * HALF, 2 * width)), probs_spec,
         by_rows(QROWS, width), by_rows(QROWS, PAIR), by_rows(QROWS, PAIR)],
        [shape((rows, width), BF16), shape((rows + 2 * HALF, 2 * width), F32)],
        [by_rows(QROWS, width), whole((rows + 2 * HALF, 2 * width))],
        2 * attend_flops,
    )
    from_below, from_above = neighbours(
        d_kv[:HALF].astype(BF16), d_kv[rows + HALF :].astype(BF16)
    )
    (d_qkv,) = call(
        finish_kernel, big, (d_q, d_kv, from_below, from_above, cosine, sine),
        [by_rows(ROWS, width), whole((rows + 2 * HALF, 2 * width)), whole((HALF, 2 * width)),
         whole((HALF, 2 * width)), by_rows(ROWS, PAIR), by_rows(ROWS, PAIR)],
        [shape((rows, 3 * width), BF16)],
        [by_rows(ROWS, 3 * width)],
        8 * rows * width,
    )
    grad_qkv = weight_grad(normed_attn, d_qkv).reshape(lines, split, -1, 3 * width)
    out_qkv = reduce_grad(grad_qkv).reshape(-1, 3 * width).astype(F32)
    d_tokens, d_gain_a = call(
        norm_back_kernel, big, (x, gain_a, d_qkv, full_qkv, d_resid),
        [by_rows(ROWS, width), whole((1, width)), by_rows(ROWS, 3 * width),
         whole((width, 3 * width)), by_rows(ROWS, width)],
        [shape((rows, width), F32), shape((1, width), F32)],
        [by_rows(ROWS, width), whole((1, width))],
        6 * rows * width * width,
    )
    gain_sums = sum_small(jnp.concatenate([d_gain_a, d_gain_m], axis=0))
    share = width // lines
    gain_own = lax.dynamic_slice_in_dim(
        gain_sums.reshape(2, lines, share), lax.axis_index("wsh"), 1, 1
    )[:, 0]
    out_in, out_attn, out_down = unpack(out_packed, rows_in, rows_attn)
    return (
        mixed[None],
        d_tokens[None],
        out_qkv,
        out_attn.astype(F32),
        out_in.astype(F32),
        out_down.astype(F32),
        gain_own[0],
        gain_own[1],
    )


def solution(mesh):
    rows = P("wsh", "seq", None)
    return jax.shard_map(
        body,
        mesh=mesh,
        in_specs=(
            rows, P("wsh", "seq"), P("wsh", None), P("wsh", None), P("wsh", None),
            P("wsh", None), P("wsh"), P("wsh"), rows,
        ),
        out_specs=(
            rows, rows, P("wsh", None), P("wsh", None), P("wsh", None), P("wsh", None),
            P("wsh"), P("wsh"),
        ),
        check_vma=False,
    )
```

```python
import functools

import jax
import jax.numpy as jnp
from jax import lax
from jax.experimental import pallas as pl
from jax.experimental.pallas import tpu as pltpu
from jax.sharding import PartitionSpec as P

HEADS = 12
HALF = 64
HEAD_DIM = 64
PAIR = 2 * HEAD_DIM
EPS = 1e-05
NEGATIVE = -1e30
QROWS = 128
ROWS = 256
SPLIT = 8
VMEM_LIMIT = 56 * 1024 * 1024
F32 = jnp.float32
BF16 = jnp.bfloat16
LAST = (((1,), (1,)), ((), ()))
FIRST = (((0,), (0,)), ((), ()))


MESH = pl.DeviceIdType.MESH


def place():
    here = lax.axis_index("seq")
    bits, partners = [], []
    for bit in (1, 2, 4):
        value = lax.rem(here // bit, 2)
        bits.append(value)
        partners.append({"seq": here + bit * (1 - 2 * value)})
    return here, bits, partners, lax.axis_index("wsh")


def greet(targets):
    barrier = pltpu.get_barrier_semaphore()
    for target in targets:
        pl.semaphore_signal(barrier, inc=1, device_id=target, device_id_type=MESH)
    pl.semaphore_wait(barrier, len(targets))


def remote(source, target, send, recv, device):
    return pltpu.make_async_remote_copy(
        src_ref=source, dst_ref=target, send_sem=send, recv_sem=recv,
        device_id=device, device_id_type=MESH,
    )


def half_lanes(ref, which):
    size = ref.shape[-1] // 2
    return pl.ds(pl.multiple_of(which * size, 128), size)


def gather_kernel(seqs, lines, arrays, *refs):
    shards, ids = refs[:arrays], refs[arrays]
    fulls = refs[arrays + 1 : 2 * arrays + 1]
    below, above = refs[2 * arrays + 1 : 2 * arrays + 3]
    sends, recvs, locals_, id_send, id_recv = refs[2 * arrays + 3 :]
    here, bits, partners, row = place()
    up = {"seq": lax.rem(here + 1, seqs)}
    down = {"seq": lax.rem(here + seqs - 1, seqs)}
    others = [{"wsh": lax.rem(row + k, lines)} for k in range(1, lines)]
    greet(partners + others + [up, down])
    moves = [
        remote(ids, below, id_send.at[0], id_recv.at[0], up),
        remote(ids, above, id_send.at[1], id_recv.at[1], down),
    ]
    for move in moves:
        move.start()
    keeps = []
    stages = [[], [], [], []]
    for a in range(arrays):
        first, second = (1, 2) if a % 2 == 0 else (2, 1)
        p, q = bits[first], bits[second]
        lanes = half_lanes(shards[a], bits[0])
        for k in range(1, lines):
            stages[0].append(
                remote(
                    shards[a].at[p, q, :, lanes], fulls[a].at[row, p, q, :, lanes],
                    sends.at[0, a, k - 1], recvs.at[0, a, k - 1], others[k - 1],
                )
            )
            origin = lax.rem(row + lines - k, lines)
            parts = (
                fulls[a].at[origin, p, q, :, lanes],
                fulls[a].at[origin, p, :, :, lanes],
                fulls[a].at[origin, :, :, :, lanes],
            )
            for stage, part, bit in zip((1, 2, 3), parts, (second, first, 0)):
                stages[stage].append(
                    remote(
                        part, part, sends.at[stage, a, k - 1], recvs.at[stage, a, k - 1],
                        partners[bit],
                    )
                )
        keeps.append(pltpu.make_async_copy(shards[a], fulls[a].at[row], locals_.at[a]))
    for move in stages[0]:
        move.start()
    for keep in keeps:
        keep.start()
    for stage in (1, 2, 3):
        for before, move in zip(stages[stage - 1], stages[stage]):
            before.wait_recv()
            move.start()
    for move in stages[3]:
        move.wait_recv()
    for stage in stages:
        for move in stage:
            move.wait_send()
    for keep in keeps:
        keep.wait()
    for move in moves:
        move.wait()


def gather_all(shards, ids, collective_id):
    seqs, lines = lax.axis_size("seq"), lax.axis_size("wsh")
    count = len(shards)
    vmem = pl.BlockSpec(memory_space=pltpu.VMEM)
    outs = [shape((lines,) + s.shape, s.dtype) for s in shards] + [shape(ids.shape, ids.dtype)] * 2
    return pl.pallas_call(
        functools.partial(gather_kernel, seqs, lines, count),
        out_shape=outs,
        in_specs=[vmem] * (count + 1),
        out_specs=[vmem] * len(outs),
        scratch_shapes=[
            pltpu.SemaphoreType.DMA((4, count, lines - 1)),
            pltpu.SemaphoreType.DMA((4, count, lines - 1)),
            pltpu.SemaphoreType.DMA((count,)),
            pltpu.SemaphoreType.DMA((2,)),
            pltpu.SemaphoreType.DMA((2,)),
        ],
        compiler_params=pltpu.CompilerParams(
            collective_id=collective_id, has_side_effects=True, vmem_limit_bytes=VMEM_LIMIT
        ),
    )(*shards, ids)


def reduce_kernel(lines, arrays, *refs):
    terms, sums = refs[:arrays], refs[arrays : 2 * arrays]
    buffers = refs[2 * arrays : 7 * arrays]
    sends, recvs = refs[7 * arrays :]
    here, bits, partners, row = place()
    others = [{"wsh": lax.rem(row + k, lines)} for k in range(1, lines)]
    greet(partners + others)
    begun = []

    def begin(move):
        move.start()
        begun.append(move)
        return move

    state = []
    for a in range(arrays):
        first, second = (1, 2) if a % 2 == 0 else (2, 1)
        p, q = bits[first], bits[second]
        total, one, two, three, cross = buffers[5 * a : 5 * a + 5]
        mine = half_lanes(terms[a], bits[0])
        theirs = half_lanes(terms[a], 1 - bits[0])
        state.append((first, second, p, q, total, one, two, three, cross, mine))
        begin(
            remote(
                terms[a].at[:, :, :, :, theirs], one, sends.at[0, a], recvs.at[0, a], partners[0]
            )
        )
    before = list(begun)
    after = []
    for a in range(arrays):
        first, second, p, q, total, one, two, three, cross, mine = state[a]
        before[a].wait_recv()

        @pl.loop(0, lines * 4)
        def _(i):
            z, u, v = i // 4, lax.rem(i // 2, 2), lax.rem(i, 2)
            total[z, u, v] = (
                terms[a][z, u, v, :, mine].astype(F32) + one[z, u, v].astype(F32)
            ).astype(BF16)

        after.append(
            begin(
                remote(
                    total.at[:, 1 - p], two, sends.at[1, a], recvs.at[1, a], partners[first]
                )
            )
        )
    before, after = after, []
    for a in range(arrays):
        first, second, p, q, total, one, two, three, cross, mine = state[a]
        before[a].wait_recv()

        @pl.loop(0, lines * 2)
        def _(i):
            z, v = i // 2, lax.rem(i, 2)
            total[z, p, v] = (total[z, p, v].astype(F32) + two[z, v].astype(F32)).astype(BF16)

        after.append(
            begin(
                remote(
                    total.at[:, p, 1 - q], three, sends.at[2, a], recvs.at[2, a], partners[second]
                )
            )
        )
    before, after = after, []
    for a in range(arrays):
        first, second, p, q, total, one, two, three, cross, mine = state[a]
        before[a].wait_recv()

        @pl.loop(0, lines)
        def _(z):
            total[z, p, q] = (total[z, p, q].astype(F32) + three[z].astype(F32)).astype(BF16)

        after.append(
            [
                begin(
                    remote(
                        total.at[lax.rem(row + k, lines), p, q], cross.at[k - 1],
                        sends.at[2 + k, a], recvs.at[2 + k, a], others[k - 1],
                    )
                )
                for k in range(1, lines)
            ]
        )
    before, after = after, []
    for a in range(arrays):
        first, second, p, q, total, one, two, three, cross, mine = state[a]
        value = total[row, p, q].astype(F32)
        for k in range(1, lines):
            before[a][k - 1].wait_recv()
            value = value + cross[k - 1].astype(F32)
        sums[a][p, q, :, mine] = value.astype(BF16)
        part = sums[a].at[p, q, :, mine]
        after.append(
            begin(
                remote(part, part, sends.at[lines + 2, a], recvs.at[lines + 2, a], partners[second])
            )
        )
    for stage, bit in ((lines + 3, 0), (lines + 4, 1)):
        before, after = after, []
        for a in range(arrays):
            first, second, p, q, total, one, two, three, cross, mine = state[a]
            before[a].wait_recv()
            part = sums[a].at[p, :, :, mine] if bit == 0 else sums[a].at[:, :, :, mine]
            target = partners[first] if bit == 0 else partners[0]
            after.append(begin(remote(part, part, sends.at[stage, a], recvs.at[stage, a], target)))
    for move in after:
        move.wait_recv()
    for move in begun:
        move.wait_send()


def reduce_all(terms, collective_id):
    lines, seqs = lax.axis_size("wsh"), lax.axis_size("seq")
    count = len(terms)
    vmem = pl.BlockSpec(memory_space=pltpu.VMEM)
    scratch = []
    for term in terms:
        r, c = term.shape[3], term.shape[4] // 2
        for lead in ((lines, 2, 2), (lines, 2, 2), (lines, 2), (lines,), (lines - 1,)):
            scratch.append(pltpu.VMEM(lead + (r, c), BF16))
    scratch += [pltpu.SemaphoreType.DMA((lines + 5, count))] * 2
    sums = pl.pallas_call(
        functools.partial(reduce_kernel, lines, count),
        out_shape=[shape(t.shape[1:], BF16) for t in terms],
        in_specs=[vmem] * count,
        out_specs=[vmem] * count,
        scratch_shapes=scratch,
        compiler_params=pltpu.CompilerParams(
            collective_id=collective_id, has_side_effects=True, vmem_limit_bytes=VMEM_LIMIT
        ),
    )(*terms)
    bit = SPLIT
    while bit < seqs:
        swaps = [(i, i ^ bit) for i in range(seqs)]
        sums = [s + lax.ppermute(s, "seq", swaps) for s in sums]
        bit *= 2
    return sums


def neighbours(low_edge, high_edge):
    count = lax.axis_size("seq")
    forward = [(i, i + 1) for i in range(count - 1)]
    backward = [(j, i) for i, j in forward]
    return lax.ppermute(high_edge, "seq", forward), lax.ppermute(low_edge, "seq", backward)


def swap(values):
    lane = lax.broadcasted_iota(jnp.int32, values.shape, 1)
    quarter = HEAD_DIM // 2
    return jnp.where(
        lane % HEAD_DIM < quarter,
        pltpu.roll(values, PAIR - quarter, 1),
        pltpu.roll(values, quarter, 1),
    )


def normalise(values):
    centre = jnp.mean(values, axis=-1, keepdims=True)
    shifted = values - centre
    factor = lax.rsqrt(jnp.mean(shifted * shifted, axis=-1, keepdims=True) + EPS)
    return shifted * factor, factor


def project_kernel(x_ref, gain_ref, w_ref, cos_ref, sin_ref, normed_ref, q_ref, kv_ref):
    width = x_ref.shape[1]
    normed, _ = normalise(x_ref[...].astype(F32))
    low = (normed * gain_ref[...].astype(F32)).astype(BF16)
    normed_ref[...] = low
    cosine, sine = cos_ref[...], sin_ref[...]
    scale = HEAD_DIM ** (-0.5)
    for part in range(2):
        raw = jnp.dot(
            low, w_ref[:, part * width : (part + 1) * width], preferred_element_type=F32
        )
        for start in range(0, width, PAIR):
            piece = raw[:, start : start + PAIR]
            turned = (piece * cosine + swap(piece) * sine).astype(BF16)
            if part == 0:
                q_ref[:, start : start + PAIR] = turned * jnp.asarray(scale, BF16)
            else:
                kv_ref[:, start : start + PAIR] = turned
    kv_ref[:, width:] = jnp.dot(
        low, w_ref[:, 2 * width :], preferred_element_type=F32
    ).astype(BF16)


def both(pair):
    lane = lax.broadcasted_iota(jnp.int32, pair.shape, 1)
    zero = jnp.zeros_like(pair)
    left = jnp.where(lane < HEAD_DIM, pair, zero)
    right = jnp.where(lane < HEAD_DIM, zero, pair)
    return jnp.concatenate([left, right], axis=0)


def merge(stacked):
    rows = stacked.shape[0] // 2
    lane = lax.broadcasted_iota(jnp.int32, (rows, stacked.shape[1]), 1)
    return jnp.where(lane < HEAD_DIM, stacked[:rows], stacked[rows:])


def attend_kernel(q_ref, kv_ref, row_ref, col_ref, context_ref, probs_ref):
    width = q_ref.shape[1]
    span = QROWS + 2 * HALF
    offset = pl.multiple_of(pl.program_id(0) * QROWS, QROWS)
    row = lax.broadcasted_iota(jnp.int32, (QROWS, span), 0)
    col = lax.broadcasted_iota(jnp.int32, (QROWS, span), 1)
    near = (col >= row) & (col <= row + 2 * HALF)
    allowed = near & (row_ref[...] == col_ref[0])
    bias = jnp.where(allowed, 0.0, NEGATIVE)
    bias = jnp.concatenate([bias, bias], axis=0)
    for pair in range(width // PAIR):
        lanes = slice(pair * PAIR, (pair + 1) * PAIR)
        queries = both(q_ref[:, lanes])
        keys = kv_ref[pl.ds(offset, span), lanes]
        values = kv_ref[pl.ds(offset, span), slice(width + pair * PAIR, width + (pair + 1) * PAIR)]
        scores = lax.dot_general(queries, keys, LAST, preferred_element_type=F32)
        scores = jnp.where(bias < 0.0, NEGATIVE, scores)
        raised = jnp.exp(scores - jnp.max(scores, axis=-1, keepdims=True))
        probs = raised * (1.0 / jnp.sum(raised, axis=-1, keepdims=True))
        low = probs.astype(BF16)
        probs_ref[0, pair] = low
        context = jnp.dot(low, values, preferred_element_type=F32)
        context_ref[:, lanes] = merge(context).astype(BF16)


def mlp_kernel(
    x_ref, context_ref, dy_ref, gain_ref, w_attn_ref, w_in_ref, w_down_ref,
    mixed_ref, normed_ref, hidden_ref, d_gate_ref, d_resid_ref, d_low_ref, d_context_ref, d_gain_ref,
):
    hidden_width = w_down_ref.shape[0]
    scales = gain_ref[...].astype(F32)
    resid = x_ref[...].astype(F32) + jnp.dot(
        context_ref[...], w_attn_ref[...], preferred_element_type=F32
    )
    normed, factor = normalise(resid)
    low = (normed * scales).astype(BF16)
    normed_ref[...] = low
    dy = dy_ref[...]
    mixed = resid
    d_normed = jnp.zeros_like(resid)
    step = hidden_width // 3
    for start in range(0, hidden_width, step):
        here = slice(start, start + step)
        there = slice(hidden_width + start, hidden_width + start + step)
        gate = jnp.dot(low, w_in_ref[:, here], preferred_element_type=F32)
        up = jnp.dot(low, w_in_ref[:, there], preferred_element_type=F32)
        d_hidden = lax.dot_general(dy, w_down_ref[here, :], LAST, preferred_element_type=F32)
        cdf = 0.5 + 0.5 * lax.erf(gate * (0.5**0.5))
        pdf = jnp.exp(-0.5 * gate * gate) * 0.3989422804014327
        gelu = gate * cdf
        hidden = (gelu * up).astype(BF16)
        hidden_ref[:, here] = hidden
        mixed = mixed + jnp.dot(hidden, w_down_ref[here, :], preferred_element_type=F32)
        d_gate = (d_hidden * up * (cdf + gate * pdf)).astype(BF16)
        d_up = (d_hidden * gelu).astype(BF16)
        d_gate_ref[:, here] = d_gate
        d_gate_ref[:, there] = d_up
        d_normed = d_normed + lax.dot_general(
            d_gate, w_in_ref[:, here], LAST, preferred_element_type=F32
        )
        d_normed = d_normed + lax.dot_general(
            d_up, w_in_ref[:, there], LAST, preferred_element_type=F32
        )
    mixed_ref[...] = mixed.astype(BF16)
    partial = jnp.sum(d_normed * normed, axis=0, keepdims=True)

    @pl.when(pl.program_id(0) == 0)
    def _():
        d_gain_ref[...] = jnp.zeros_like(d_gain_ref)

    d_gain_ref[...] += partial
    scaled = d_normed * scales
    mean = jnp.mean(scaled, axis=-1, keepdims=True)
    cross = jnp.mean(scaled * normed, axis=-1, keepdims=True)
    d_resid = dy.astype(F32) + factor * (scaled - mean - normed * cross)
    d_resid_ref[...] = d_resid
    d_low = d_resid.astype(BF16)
    d_low_ref[...] = d_low
    d_context_ref[...] = lax.dot_general(
        d_low, w_attn_ref[...], LAST, preferred_element_type=F32
    ).astype(BF16)


def attend_back_kernel(
    q_ref, kv_ref, probs_ref, d_ref, cos_ref, sin_ref, d_q_ref, d_kv_ref
):
    width = q_ref.shape[1]
    span = QROWS + 2 * HALF
    offset = pl.multiple_of(pl.program_id(0) * QROWS, QROWS)

    @pl.when(pl.program_id(0) == 0)
    def _():
        d_kv_ref[...] = jnp.zeros_like(d_kv_ref)

    cosine, sine = cos_ref[...], sin_ref[...]
    scale = HEAD_DIM ** (-0.5)
    for pair in range(width // PAIR):
        lanes = slice(pair * PAIR, (pair + 1) * PAIR)
        value_lanes = slice(width + pair * PAIR, width + (pair + 1) * PAIR)
        queries = both(q_ref[:, lanes])
        d_out = both(d_ref[:, lanes])
        keys = kv_ref[pl.ds(offset, span), lanes]
        values = kv_ref[pl.ds(offset, span), value_lanes]
        low = probs_ref[0, pair]
        probs = low.astype(F32)
        d_probs = lax.dot_general(d_out, values, LAST, preferred_element_type=F32)
        delta = jnp.sum(d_probs * probs, axis=-1, keepdims=True)
        d_scores = (probs * (d_probs - delta)).astype(BF16)
        d_kv_ref[pl.ds(offset, span), value_lanes] += lax.dot_general(
            low, d_out, FIRST, preferred_element_type=F32
        )
        d_kv_ref[pl.ds(offset, span), lanes] += lax.dot_general(
            d_scores, queries, FIRST, preferred_element_type=F32
        )
        d_q = merge(jnp.dot(d_scores, keys, preferred_element_type=F32)) * scale
        d_q_ref[:, lanes] = (d_q * cosine - swap(d_q) * sine).astype(BF16)


def finish_kernel(d_q_ref, d_kv_ref, low_ref, high_ref, cos_ref, sin_ref, d_qkv_ref):
    width = d_q_ref.shape[1]
    step = pl.program_id(0)
    offset = pl.multiple_of(step * ROWS, ROWS)
    first = step == 0
    last = step == pl.num_programs(0) - 1
    cosine, sine = cos_ref[...], sin_ref[...]
    d_qkv_ref[:, :width] = d_q_ref[...]
    for start in range(0, 2 * width, PAIR):
        lanes = slice(start, start + PAIR)
        block = d_kv_ref[pl.ds(offset + HALF, ROWS), lanes]
        low = jnp.where(first, low_ref[:, lanes].astype(F32), 0.0)
        high = jnp.where(last, high_ref[:, lanes].astype(F32), 0.0)
        block = jnp.concatenate(
            [block[:HALF] + low, block[HALF : ROWS - HALF], block[ROWS - HALF :] + high], axis=0
        )
        if start < width:
            block = block * cosine - swap(block) * sine
        d_qkv_ref[:, width + start : width + start + PAIR] = block.astype(BF16)


def norm_back_kernel(x_ref, gain_ref, d_qkv_ref, w_ref, d_resid_ref, d_tokens_ref, d_gain_ref):
    normed, factor = normalise(x_ref[...].astype(F32))
    d_normed = lax.dot_general(d_qkv_ref[...], w_ref[...], LAST, preferred_element_type=F32)
    partial = jnp.sum(d_normed * normed, axis=0, keepdims=True)

    @pl.when(pl.program_id(0) == 0)
    def _():
        d_gain_ref[...] = jnp.zeros_like(d_gain_ref)

    d_gain_ref[...] += partial
    scaled = d_normed * gain_ref[...].astype(F32)
    mean = jnp.mean(scaled, axis=-1, keepdims=True)
    cross = jnp.mean(scaled * normed, axis=-1, keepdims=True)
    d_tokens_ref[...] = d_resid_ref[...] + factor * (scaled - mean - normed * cross)


def by_rows(rows, width):
    return pl.BlockSpec((rows, width), lambda i: (i, 0))


def whole(shape):
    return pl.BlockSpec(shape, lambda i: (0,) * len(shape))


def call(kernel, steps, inputs, specs, outs, out_specs, flops):
    size = sum(a.size * a.dtype.itemsize for a in inputs)
    size += sum(o.size * o.dtype.itemsize for o in outs)
    return pl.pallas_call(
        kernel,
        grid=(steps,),
        in_specs=specs,
        out_specs=out_specs,
        out_shape=outs,
        compiler_params=pltpu.CompilerParams(
            dimension_semantics=("arbitrary",), vmem_limit_bytes=VMEM_LIMIT
        ),
        cost_estimate=pl.CostEstimate(flops=flops, bytes_accessed=size, transcendentals=0),
    )(*inputs)


def shape(dims, dtype):
    return jax.ShapeDtypeStruct(dims, dtype)


def body(tokens, positions, w_qkv, w_attn, w_in, w_down, gain_attn, gain_mlp, grad_out):
    rows, width = tokens.shape[1:]
    lines = lax.axis_size("wsh")
    hidden = w_down.shape[0] * lines
    x = tokens[0]
    dy = grad_out[0]
    places = positions[0]
    seq = lax.axis_index("seq")
    seqs = lax.axis_size("seq")

    share = width // lines
    quarter_rows = w_down.shape[0] // 4

    def quarters(array, lead=()):
        return array.reshape(lead + (2, 2, -1, array.shape[-1]))

    def with_gains(down, attn_scale, mlp_scale, lead):
        extra = jnp.stack([attn_scale.reshape(lead + (4, -1)), mlp_scale.reshape(lead + (4, -1))], axis=-2)
        pads = [(0, 0)] * (len(lead) + 1) + [(0, 6), (0, width - extra.shape[-1])]
        joined = jnp.concatenate(
            [down.astype(F32).reshape(lead + (4, quarter_rows, width)), jnp.pad(extra.astype(F32), pads)],
            axis=-2,
        )
        return quarters(joined.reshape(lead + (-1, width)).astype(BF16), lead)

    base = seq * rows
    ids = places - (base + jnp.arange(rows, dtype=jnp.int32))
    full_qkv, full_in, full_attn, full_down, ids_below, ids_above = gather_all(
        (quarters(w_qkv), quarters(w_in), quarters(w_attn),
         with_gains(w_down, gain_attn, gain_mlp, ())),
        ids.reshape(-1, 128), 0,
    )
    full_qkv = full_qkv.reshape(width, 3 * width)
    full_in = full_in.reshape(width, 2 * hidden)
    full_attn = full_attn.reshape(width, width)
    blocks_down = full_down.reshape(lines, 4, -1, width)
    full_down = blocks_down[:, :, :quarter_rows].reshape(hidden, width)
    gain_a = blocks_down[:, :, quarter_rows, : share // 4].reshape(1, width)
    gain_m = blocks_down[:, :, quarter_rows + 1, : share // 4].reshape(1, width)
    below = ids_below.reshape(-1)[rows - HALF :]
    above = ids_above.reshape(-1)[:HALF]
    nowhere = jnp.int32(-(1 << 30))
    below = jnp.where(seq == 0, nowhere, below)
    above = jnp.where(seq == seqs - 1, nowhere, above)
    ids_wide = jnp.concatenate([below, ids, above])
    blocks = rows // QROWS
    span = QROWS + 2 * HALF
    cols = jnp.stack([ids_wide[i * QROWS : i * QROWS + span] for i in range(blocks)])[:, None, :]

    lane = jnp.arange(PAIR, dtype=jnp.int32)
    quarter = HEAD_DIM // 2
    exponent = (lane % quarter).astype(F32) * (2.0 / HEAD_DIM)
    frequency = jnp.power(F32(10000.0), -exponent)
    angles = places.astype(F32)[:, None] * frequency[None, :]
    cosine = jnp.cos(angles)
    sine = jnp.where(lane % HEAD_DIM < quarter, -1.0, 1.0)[None, :] * jnp.sin(angles)

    big = rows // ROWS
    normed_attn, queries, kv = call(
        project_kernel, big, (x, gain_a, full_qkv, cosine, sine),
        [by_rows(ROWS, width), whole((1, width)), whole((width, 3 * width)),
         by_rows(ROWS, PAIR), by_rows(ROWS, PAIR)],
        [shape((rows, width), BF16), shape((rows, width), BF16), shape((rows, 2 * width), BF16)],
        [by_rows(ROWS, width), by_rows(ROWS, width), by_rows(ROWS, 2 * width)],
        6 * rows * width * width,
    )
    kv_below, kv_above = neighbours(kv[:HALF], kv[rows - HALF :])
    kv_wide = jnp.concatenate([kv_below, kv, kv_above], axis=0)
    pairs = width // PAIR
    probs_spec = pl.BlockSpec((1, pairs, 2 * QROWS, span), lambda i: (i, 0, 0, 0))
    attend_flops = 4 * blocks * pairs * 2 * QROWS * span * PAIR
    context, probs = call(
        attend_kernel, blocks, (queries, kv_wide, ids[:, None], cols),
        [by_rows(QROWS, width), whole((rows + 2 * HALF, 2 * width)), by_rows(QROWS, 1),
         pl.BlockSpec((1, 1, span), lambda i: (i, 0, 0))],
        [shape((rows, width), BF16), shape((blocks, pairs, 2 * QROWS, span), BF16)],
        [by_rows(QROWS, width), probs_spec],
        attend_flops,
    )
    mixed, normed_mlp, hidden_low, d_gate, d_resid, d_low, d_context, d_gain_m = call(
        mlp_kernel, big, (x, context, dy, gain_m, full_attn, full_in, full_down),
        [by_rows(ROWS, width), by_rows(ROWS, width), by_rows(ROWS, width), whole((1, width)),
         whole((width, width)), whole((width, 2 * hidden)), whole((hidden, width))],
        [shape((rows, width), BF16), shape((rows, width), BF16), shape((rows, hidden), BF16),
         shape((rows, 2 * hidden), BF16), shape((rows, width), F32), shape((rows, width), BF16),
         shape((rows, width), BF16), shape((1, width), F32)],
        [by_rows(ROWS, width), by_rows(ROWS, width), by_rows(ROWS, hidden),
         by_rows(ROWS, 2 * hidden), by_rows(ROWS, width), by_rows(ROWS, width),
         by_rows(ROWS, width), whole((1, width))],
        2 * rows * width * (2 * width + 6 * hidden),
    )

    def weight_grad(left, right):
        return lax.dot_general(left, right, FIRST, preferred_element_type=F32).astype(BF16)

    grad_in = weight_grad(normed_mlp, d_gate)
    grad_attn = weight_grad(context, d_low)
    grad_down = lax.dot_general(hidden_low, dy, FIRST, preferred_element_type=F32)

    d_q, d_kv = call(
        attend_back_kernel, blocks, (queries, kv_wide, probs, d_context, cosine, sine),
        [by_rows(QROWS, width), whole((rows + 2 * HALF, 2 * width)), probs_spec,
         by_rows(QROWS, width), by_rows(QROWS, PAIR), by_rows(QROWS, PAIR)],
        [shape((rows, width), BF16), shape((rows + 2 * HALF, 2 * width), F32)],
        [by_rows(QROWS, width), whole((rows + 2 * HALF, 2 * width))],
        2 * attend_flops,
    )
    from_below, from_above = neighbours(
        d_kv[:HALF].astype(BF16), d_kv[rows + HALF :].astype(BF16)
    )
    (d_qkv,) = call(
        finish_kernel, big, (d_q, d_kv, from_below, from_above, cosine, sine),
        [by_rows(ROWS, width), whole((rows + 2 * HALF, 2 * width)), whole((HALF, 2 * width)),
         whole((HALF, 2 * width)), by_rows(ROWS, PAIR), by_rows(ROWS, PAIR)],
        [shape((rows, 3 * width), BF16)],
        [by_rows(ROWS, 3 * width)],
        8 * rows * width,
    )
    grad_qkv = weight_grad(normed_attn, d_qkv)
    d_tokens, d_gain_a = call(
        norm_back_kernel, big, (x, gain_a, d_qkv, full_qkv, d_resid),
        [by_rows(ROWS, width), whole((1, width)), by_rows(ROWS, 3 * width),
         whole((width, 3 * width)), by_rows(ROWS, width)],
        [shape((rows, width), F32), shape((1, width), F32)],
        [by_rows(ROWS, width), whole((1, width))],
        6 * rows * width * width,
    )
    lead = (lines,)
    out_qkv, out_in, out_attn, out_down = reduce_all(
        (quarters(grad_qkv, lead), quarters(grad_in, lead), quarters(grad_attn, lead),
         with_gains(grad_down, d_gain_a[0], d_gain_m[0], lead)),
        1,
    )
    out_down = out_down.reshape(4, -1, width)
    return (
        mixed[None],
        d_tokens[None],
        out_qkv.reshape(share, 3 * width).astype(F32),
        out_attn.reshape(share, width).astype(F32),
        out_in.reshape(share, 2 * hidden).astype(F32),
        out_down[:, :quarter_rows].reshape(-1, width).astype(F32),
        out_down[:, quarter_rows, : share // 4].reshape(-1).astype(F32),
        out_down[:, quarter_rows + 1, : share // 4].reshape(-1).astype(F32),
    )


def solution(mesh):
    rows = P("wsh", "seq", None)
    return jax.shard_map(
        body,
        mesh=mesh,
        in_specs=(
            rows, P("wsh", "seq"), P("wsh", None), P("wsh", None), P("wsh", None),
            P("wsh", None), P("wsh"), P("wsh"), rows,
        ),
        out_specs=(
            rows, rows, P("wsh", None), P("wsh", None), P("wsh", None), P("wsh", None),
            P("wsh"), P("wsh"),
        ),
        check_vma=False,
    )
```

```python
import functools

import jax
import jax.numpy as jnp
from jax import lax
from jax.experimental import pallas as pl
from jax.experimental.pallas import tpu as pltpu
from jax.sharding import PartitionSpec as P

HEADS = 12
HALF = 64
HEAD_DIM = 64
PAIR = 2 * HEAD_DIM
EPS = 1e-05
NEGATIVE = -1e30
QROWS = 128
ROWS = 256
SPLIT = 8
VMEM_LIMIT = 56 * 1024 * 1024
F32 = jnp.float32
BF16 = jnp.bfloat16
LAST = (((1,), (1,)), ((), ()))
FIRST = (((0,), (0,)), ((), ()))


MESH = pl.DeviceIdType.MESH


def place():
    here = lax.axis_index("seq")
    bits, partners = [], []
    for bit in (1, 2, 4):
        value = lax.rem(here // bit, 2)
        bits.append(value)
        partners.append({"seq": here + bit * (1 - 2 * value)})
    return here, bits, partners, lax.axis_index("wsh")


def greet(targets):
    barrier = pltpu.get_barrier_semaphore()
    for target in targets:
        pl.semaphore_signal(barrier, inc=1, device_id=target, device_id_type=MESH)
    pl.semaphore_wait(barrier, len(targets))


def remote(source, target, send, recv, device):
    return pltpu.make_async_remote_copy(
        src_ref=source, dst_ref=target, send_sem=send, recv_sem=recv,
        device_id=device, device_id_type=MESH,
    )


def half_lanes(ref, which):
    size = ref.shape[-1] // 2
    return pl.ds(pl.multiple_of(which * size, 128), size)


def gather_kernel(seqs, lines, arrays, *refs):
    shards, ids = refs[:arrays], refs[arrays]
    fulls = refs[arrays + 1 : 2 * arrays + 1]
    below, above = refs[2 * arrays + 1 : 2 * arrays + 3]
    sends, recvs, locals_, id_send, id_recv = refs[2 * arrays + 3 :]
    here, bits, partners, row = place()
    up = {"seq": lax.rem(here + 1, seqs)}
    down = {"seq": lax.rem(here + seqs - 1, seqs)}
    others = [{"wsh": lax.rem(row + k, lines)} for k in range(1, lines)]
    greet(partners + others + [up, down])
    moves = [
        remote(ids, below, id_send.at[0], id_recv.at[0], up),
        remote(ids, above, id_send.at[1], id_recv.at[1], down),
    ]
    for move in moves:
        move.start()
    keeps = []
    stages = [[], [], [], []]
    for a in range(arrays):
        first, second = (1, 2) if a % 2 == 0 else (2, 1)
        p, q = bits[first], bits[second]
        lanes = half_lanes(shards[a], bits[0])
        for k in range(1, lines):
            stages[0].append(
                remote(
                    shards[a].at[p, q, :, lanes], fulls[a].at[row, p, q, :, lanes],
                    sends.at[0, a, k - 1], recvs.at[0, a, k - 1], others[k - 1],
                )
            )
            origin = lax.rem(row + lines - k, lines)
            parts = (
                fulls[a].at[origin, p, q, :, lanes],
                fulls[a].at[origin, p, :, :, lanes],
                fulls[a].at[origin, :, :, :, lanes],
            )
            for stage, part, bit in zip((1, 2, 3), parts, (second, first, 0)):
                stages[stage].append(
                    remote(
                        part, part, sends.at[stage, a, k - 1], recvs.at[stage, a, k - 1],
                        partners[bit],
                    )
                )
        keeps.append(pltpu.make_async_copy(shards[a], fulls[a].at[row], locals_.at[a]))
    for move in stages[0]:
        move.start()
    for keep in keeps:
        keep.start()
    for stage in (1, 2, 3):
        for before, move in zip(stages[stage - 1], stages[stage]):
            before.wait_recv()
            move.start()
    for move in stages[3]:
        move.wait_recv()
    for stage in stages:
        for move in stage:
            move.wait_send()
    for keep in keeps:
        keep.wait()
    for move in moves:
        move.wait()


def gather_all(shards, ids, collective_id):
    seqs, lines = lax.axis_size("seq"), lax.axis_size("wsh")
    count = len(shards)
    vmem = pl.BlockSpec(memory_space=pltpu.VMEM)
    outs = [shape((lines,) + s.shape, s.dtype) for s in shards] + [shape(ids.shape, ids.dtype)] * 2
    return pl.pallas_call(
        functools.partial(gather_kernel, seqs, lines, count),
        out_shape=outs,
        in_specs=[vmem] * (count + 1),
        out_specs=[vmem] * len(outs),
        scratch_shapes=[
            pltpu.SemaphoreType.DMA((4, count, lines - 1)),
            pltpu.SemaphoreType.DMA((4, count, lines - 1)),
            pltpu.SemaphoreType.DMA((count,)),
            pltpu.SemaphoreType.DMA((2,)),
            pltpu.SemaphoreType.DMA((2,)),
        ],
        compiler_params=pltpu.CompilerParams(
            collective_id=collective_id, has_side_effects=True, vmem_limit_bytes=VMEM_LIMIT
        ),
    )(*shards, ids)


def reduce_kernel(lines, arrays, extra_in, extra_out, work, *refs):
    terms, ins = refs[:arrays], refs[arrays : arrays + extra_in]
    refs = refs[arrays + extra_in :]
    sums, outs = refs[:arrays], refs[arrays : arrays + extra_out]
    refs = refs[arrays + extra_out :]
    buffers = refs[: 5 * arrays]
    sends, recvs = refs[5 * arrays :]
    here, bits, partners, row = place()
    others = [{"wsh": lax.rem(row + k, lines)} for k in range(1, lines)]
    greet(partners + others)
    begun = []

    def begin(move):
        move.start()
        begun.append(move)
        return move

    state = []
    for a in range(arrays):
        first, second = (1, 2) if a % 2 == 0 else (2, 1)
        p, q = bits[first], bits[second]
        total, one, two, three, cross = buffers[5 * a : 5 * a + 5]
        mine = half_lanes(terms[a], bits[0])
        theirs = half_lanes(terms[a], 1 - bits[0])
        state.append((first, second, p, q, total, one, two, three, cross, mine))
        begin(
            remote(
                terms[a].at[:, :, :, :, theirs], one, sends.at[0, a], recvs.at[0, a], partners[0]
            )
        )
    before = list(begun)
    after = []
    if work is not None:
        work(0, *ins, *outs)
    for a in range(arrays):
        first, second, p, q, total, one, two, three, cross, mine = state[a]
        before[a].wait_recv()

        @pl.loop(0, lines * 4)
        def _(i):
            z, u, v = i // 4, lax.rem(i // 2, 2), lax.rem(i, 2)
            total[z, u, v] = (
                terms[a][z, u, v, :, mine].astype(F32) + one[z, u, v].astype(F32)
            ).astype(BF16)

        after.append(
            begin(
                remote(
                    total.at[:, 1 - p], two, sends.at[1, a], recvs.at[1, a], partners[first]
                )
            )
        )
    if work is not None:
        work(1, *ins, *outs)
    before, after = after, []
    for a in range(arrays):
        first, second, p, q, total, one, two, three, cross, mine = state[a]
        before[a].wait_recv()

        @pl.loop(0, lines * 2)
        def _(i):
            z, v = i // 2, lax.rem(i, 2)
            total[z, p, v] = (total[z, p, v].astype(F32) + two[z, v].astype(F32)).astype(BF16)

        after.append(
            begin(
                remote(
                    total.at[:, p, 1 - q], three, sends.at[2, a], recvs.at[2, a], partners[second]
                )
            )
        )
    before, after = after, []
    for a in range(arrays):
        first, second, p, q, total, one, two, three, cross, mine = state[a]
        before[a].wait_recv()

        @pl.loop(0, lines)
        def _(z):
            total[z, p, q] = (total[z, p, q].astype(F32) + three[z].astype(F32)).astype(BF16)

        after.append(
            [
                begin(
                    remote(
                        total.at[lax.rem(row + k, lines), p, q], cross.at[k - 1],
                        sends.at[2 + k, a], recvs.at[2 + k, a], others[k - 1],
                    )
                )
                for k in range(1, lines)
            ]
        )
    before, after = after, []
    for a in range(arrays):
        first, second, p, q, total, one, two, three, cross, mine = state[a]
        value = total[row, p, q].astype(F32)
        for k in range(1, lines):
            before[a][k - 1].wait_recv()
            value = value + cross[k - 1].astype(F32)
        sums[a][p, q, :, mine] = value.astype(BF16)
        part = sums[a].at[p, q, :, mine]
        after.append(
            begin(
                remote(part, part, sends.at[lines + 2, a], recvs.at[lines + 2, a], partners[second])
            )
        )
    for stage, bit in ((lines + 3, 0), (lines + 4, 1)):
        before, after = after, []
        for a in range(arrays):
            first, second, p, q, total, one, two, three, cross, mine = state[a]
            before[a].wait_recv()
            part = sums[a].at[p, :, :, mine] if bit == 0 else sums[a].at[:, :, :, mine]
            target = partners[first] if bit == 0 else partners[0]
            after.append(begin(remote(part, part, sends.at[stage, a], recvs.at[stage, a], target)))
    for move in after:
        move.wait_recv()
    for move in begun:
        move.wait_send()


def reduce_all(terms, collective_id, work=None, work_in=(), work_out=()):
    lines, seqs = lax.axis_size("wsh"), lax.axis_size("seq")
    count = len(terms)
    vmem = pl.BlockSpec(memory_space=pltpu.VMEM)
    scratch = []
    for term in terms:
        r, c = term.shape[3], term.shape[4] // 2
        for lead in ((lines, 2, 2), (lines, 2, 2), (lines, 2), (lines,), (lines - 1,)):
            scratch.append(pltpu.VMEM(lead + (r, c), BF16))
    scratch += [pltpu.SemaphoreType.DMA((lines + 5, count))] * 2
    sums = pl.pallas_call(
        functools.partial(reduce_kernel, lines, count, len(work_in), len(work_out), work),
        out_shape=[shape(t.shape[1:], BF16) for t in terms] + list(work_out),
        in_specs=[vmem] * (count + len(work_in)),
        out_specs=[vmem] * (count + len(work_out)),
        scratch_shapes=scratch,
        compiler_params=pltpu.CompilerParams(
            collective_id=collective_id, has_side_effects=True, vmem_limit_bytes=VMEM_LIMIT
        ),
    )(*terms, *work_in)
    sums, made = sums[:count], sums[count:]
    bit = SPLIT
    while bit < seqs:
        swaps = [(i, i ^ bit) for i in range(seqs)]
        sums = [s + lax.ppermute(s, "seq", swaps) for s in sums]
        bit *= 2
    return list(sums), made


def neighbours(low_edge, high_edge):
    count = lax.axis_size("seq")
    forward = [(i, i + 1) for i in range(count - 1)]
    backward = [(j, i) for i, j in forward]
    return lax.ppermute(high_edge, "seq", forward), lax.ppermute(low_edge, "seq", backward)


def swap(values):
    lane = lax.broadcasted_iota(jnp.int32, values.shape, 1)
    quarter = HEAD_DIM // 2
    return jnp.where(
        lane % HEAD_DIM < quarter,
        pltpu.roll(values, PAIR - quarter, 1),
        pltpu.roll(values, quarter, 1),
    )


def normalise(values):
    centre = jnp.mean(values, axis=-1, keepdims=True)
    shifted = values - centre
    factor = lax.rsqrt(jnp.mean(shifted * shifted, axis=-1, keepdims=True) + EPS)
    return shifted * factor, factor


def project_kernel(x_ref, gain_ref, w_ref, cos_ref, sin_ref, normed_ref, q_ref, kv_ref):
    width = x_ref.shape[1]
    normed, _ = normalise(x_ref[...].astype(F32))
    low = (normed * gain_ref[...].astype(F32)).astype(BF16)
    normed_ref[...] = low
    cosine, sine = cos_ref[...], sin_ref[...]
    scale = HEAD_DIM ** (-0.5)
    for part in range(2):
        raw = jnp.dot(
            low, w_ref[:, part * width : (part + 1) * width], preferred_element_type=F32
        )
        for start in range(0, width, PAIR):
            piece = raw[:, start : start + PAIR]
            turned = (piece * cosine + swap(piece) * sine).astype(BF16)
            if part == 0:
                q_ref[:, start : start + PAIR] = turned * jnp.asarray(scale, BF16)
            else:
                kv_ref[:, start : start + PAIR] = turned
    kv_ref[:, width:] = jnp.dot(
        low, w_ref[:, 2 * width :], preferred_element_type=F32
    ).astype(BF16)


def both(pair):
    lane = lax.broadcasted_iota(jnp.int32, pair.shape, 1)
    zero = jnp.zeros_like(pair)
    left = jnp.where(lane < HEAD_DIM, pair, zero)
    right = jnp.where(lane < HEAD_DIM, zero, pair)
    return jnp.concatenate([left, right], axis=0)


def merge(stacked):
    rows = stacked.shape[0] // 2
    lane = lax.broadcasted_iota(jnp.int32, (rows, stacked.shape[1]), 1)
    return jnp.where(lane < HEAD_DIM, stacked[:rows], stacked[rows:])


def attend_kernel(q_ref, kv_ref, row_ref, col_ref, context_ref, probs_ref):
    width = q_ref.shape[1]
    span = QROWS + 2 * HALF
    offset = pl.multiple_of(pl.program_id(0) * QROWS, QROWS)
    row = lax.broadcasted_iota(jnp.int32, (QROWS, span), 0)
    col = lax.broadcasted_iota(jnp.int32, (QROWS, span), 1)
    near = (col >= row) & (col <= row + 2 * HALF)
    allowed = near & (row_ref[...] == col_ref[0])
    bias = jnp.where(allowed, 0.0, NEGATIVE)
    bias = jnp.concatenate([bias, bias], axis=0)
    for pair in range(width // PAIR):
        lanes = slice(pair * PAIR, (pair + 1) * PAIR)
        queries = both(q_ref[:, lanes])
        keys = kv_ref[pl.ds(offset, span), lanes]
        values = kv_ref[pl.ds(offset, span), slice(width + pair * PAIR, width + (pair + 1) * PAIR)]
        scores = lax.dot_general(queries, keys, LAST, preferred_element_type=F32)
        scores = jnp.where(bias < 0.0, NEGATIVE, scores)
        raised = jnp.exp(scores - jnp.max(scores, axis=-1, keepdims=True))
        probs = raised * (1.0 / jnp.sum(raised, axis=-1, keepdims=True))
        low = probs.astype(BF16)
        probs_ref[0, pair] = low
        context = jnp.dot(low, values, preferred_element_type=F32)
        context_ref[:, lanes] = merge(context).astype(BF16)


def mlp_kernel(
    x_ref, context_ref, dy_ref, gain_ref, w_attn_ref, w_in_ref, w_down_ref,
    mixed_ref, normed_ref, hidden_ref, d_gate_ref, d_resid_ref, d_low_ref, d_context_ref, d_gain_ref,
):
    hidden_width = w_down_ref.shape[0]
    scales = gain_ref[...].astype(F32)
    resid = x_ref[...].astype(F32) + jnp.dot(
        context_ref[...], w_attn_ref[...], preferred_element_type=F32
    )
    normed, factor = normalise(resid)
    low = (normed * scales).astype(BF16)
    normed_ref[...] = low
    dy = dy_ref[...]
    mixed = resid
    d_normed = jnp.zeros_like(resid)
    step = hidden_width // 3
    for start in range(0, hidden_width, step):
        here = slice(start, start + step)
        there = slice(hidden_width + start, hidden_width + start + step)
        gate = jnp.dot(low, w_in_ref[:, here], preferred_element_type=F32)
        up = jnp.dot(low, w_in_ref[:, there], preferred_element_type=F32)
        d_hidden = lax.dot_general(dy, w_down_ref[here, :], LAST, preferred_element_type=F32)
        cdf = 0.5 + 0.5 * lax.erf(gate * (0.5**0.5))
        pdf = jnp.exp(-0.5 * gate * gate) * 0.3989422804014327
        gelu = gate * cdf
        hidden = (gelu * up).astype(BF16)
        hidden_ref[:, here] = hidden
        mixed = mixed + jnp.dot(hidden, w_down_ref[here, :], preferred_element_type=F32)
        d_gate = (d_hidden * up * (cdf + gate * pdf)).astype(BF16)
        d_up = (d_hidden * gelu).astype(BF16)
        d_gate_ref[:, here] = d_gate
        d_gate_ref[:, there] = d_up
        d_normed = d_normed + lax.dot_general(
            d_gate, w_in_ref[:, here], LAST, preferred_element_type=F32
        )
        d_normed = d_normed + lax.dot_general(
            d_up, w_in_ref[:, there], LAST, preferred_element_type=F32
        )
    mixed_ref[...] = mixed.astype(BF16)
    partial = jnp.sum(d_normed * normed, axis=0, keepdims=True)

    @pl.when(pl.program_id(0) == 0)
    def _():
        d_gain_ref[...] = jnp.zeros_like(d_gain_ref)

    d_gain_ref[...] += partial
    scaled = d_normed * scales
    mean = jnp.mean(scaled, axis=-1, keepdims=True)
    cross = jnp.mean(scaled * normed, axis=-1, keepdims=True)
    d_resid = dy.astype(F32) + factor * (scaled - mean - normed * cross)
    d_resid_ref[...] = d_resid
    d_low = d_resid.astype(BF16)
    d_low_ref[...] = d_low
    d_context_ref[...] = lax.dot_general(
        d_low, w_attn_ref[...], LAST, preferred_element_type=F32
    ).astype(BF16)


def attend_back(part, q_ref, kv_ref, probs_ref, d_ref, cos_ref, sin_ref, d_q_ref, d_kv_ref):
    blocks = probs_ref.shape[0]
    cut = 3 * blocks // 8
    if part == 0:
        d_kv_ref[...] = jnp.zeros_like(d_kv_ref)

    @pl.loop(*((0, cut) if part == 0 else (cut, blocks)))
    def _(step):
        attend_back_block(
            step, q_ref, kv_ref, probs_ref, d_ref, cos_ref, sin_ref, d_q_ref, d_kv_ref
        )


def attend_back_block(
    step, q_ref, kv_ref, probs_ref, d_ref, cos_ref, sin_ref, d_q_ref, d_kv_ref
):
    width = q_ref.shape[1]
    span = QROWS + 2 * HALF
    offset = pl.multiple_of(step * QROWS, QROWS)
    rows = pl.ds(offset, QROWS)
    cosine, sine = cos_ref[rows, :], sin_ref[rows, :]
    scale = HEAD_DIM ** (-0.5)
    for pair in range(width // PAIR):
        lanes = slice(pair * PAIR, (pair + 1) * PAIR)
        value_lanes = slice(width + pair * PAIR, width + (pair + 1) * PAIR)
        queries = both(q_ref[rows, lanes])
        d_out = both(d_ref[rows, lanes])
        keys = kv_ref[pl.ds(offset, span), lanes]
        values = kv_ref[pl.ds(offset, span), value_lanes]
        low = probs_ref[step, pair]
        probs = low.astype(F32)
        d_probs = lax.dot_general(d_out, values, LAST, preferred_element_type=F32)
        delta = jnp.sum(d_probs * probs, axis=-1, keepdims=True)
        d_scores = (probs * (d_probs - delta)).astype(BF16)
        d_kv_ref[pl.ds(offset, span), value_lanes] += lax.dot_general(
            low, d_out, FIRST, preferred_element_type=F32
        )
        d_kv_ref[pl.ds(offset, span), lanes] += lax.dot_general(
            d_scores, queries, FIRST, preferred_element_type=F32
        )
        d_q = merge(jnp.dot(d_scores, keys, preferred_element_type=F32)) * scale
        d_q_ref[rows, lanes] = (d_q * cosine - swap(d_q) * sine).astype(BF16)


def finish_kernel(d_q_ref, d_kv_ref, low_ref, high_ref, cos_ref, sin_ref, d_qkv_ref):
    width = d_q_ref.shape[1]
    step = pl.program_id(0)
    offset = pl.multiple_of(step * ROWS, ROWS)
    first = step == 0
    last = step == pl.num_programs(0) - 1
    cosine, sine = cos_ref[...], sin_ref[...]
    d_qkv_ref[:, :width] = d_q_ref[...]
    for start in range(0, 2 * width, PAIR):
        lanes = slice(start, start + PAIR)
        block = d_kv_ref[pl.ds(offset + HALF, ROWS), lanes]
        low = jnp.where(first, low_ref[:, lanes].astype(F32), 0.0)
        high = jnp.where(last, high_ref[:, lanes].astype(F32), 0.0)
        block = jnp.concatenate(
            [block[:HALF] + low, block[HALF : ROWS - HALF], block[ROWS - HALF :] + high], axis=0
        )
        if start < width:
            block = block * cosine - swap(block) * sine
        d_qkv_ref[:, width + start : width + start + PAIR] = block.astype(BF16)


def norm_back_kernel(x_ref, gain_ref, d_qkv_ref, w_ref, d_resid_ref, d_tokens_ref, d_gain_ref):
    normed, factor = normalise(x_ref[...].astype(F32))
    d_normed = lax.dot_general(d_qkv_ref[...], w_ref[...], LAST, preferred_element_type=F32)
    partial = jnp.sum(d_normed * normed, axis=0, keepdims=True)

    @pl.when(pl.program_id(0) == 0)
    def _():
        d_gain_ref[...] = jnp.zeros_like(d_gain_ref)

    d_gain_ref[...] += partial
    scaled = d_normed * gain_ref[...].astype(F32)
    mean = jnp.mean(scaled, axis=-1, keepdims=True)
    cross = jnp.mean(scaled * normed, axis=-1, keepdims=True)
    d_tokens_ref[...] = d_resid_ref[...] + factor * (scaled - mean - normed * cross)


def by_rows(rows, width):
    return pl.BlockSpec((rows, width), lambda i: (i, 0))


def whole(shape):
    return pl.BlockSpec(shape, lambda i: (0,) * len(shape))


def call(kernel, steps, inputs, specs, outs, out_specs, flops):
    size = sum(a.size * a.dtype.itemsize for a in inputs)
    size += sum(o.size * o.dtype.itemsize for o in outs)
    return pl.pallas_call(
        kernel,
        grid=(steps,),
        in_specs=specs,
        out_specs=out_specs,
        out_shape=outs,
        compiler_params=pltpu.CompilerParams(
            dimension_semantics=("arbitrary",), vmem_limit_bytes=VMEM_LIMIT
        ),
        cost_estimate=pl.CostEstimate(flops=flops, bytes_accessed=size, transcendentals=0),
    )(*inputs)


def shape(dims, dtype):
    return jax.ShapeDtypeStruct(dims, dtype)


def body(tokens, positions, w_qkv, w_attn, w_in, w_down, gain_attn, gain_mlp, grad_out):
    rows, width = tokens.shape[1:]
    lines = lax.axis_size("wsh")
    hidden = w_down.shape[0] * lines
    x = tokens[0]
    dy = grad_out[0]
    places = positions[0]
    seq = lax.axis_index("seq")
    seqs = lax.axis_size("seq")

    share = width // lines
    quarter_rows = w_down.shape[0] // 4

    def quarters(array, lead=()):
        return array.reshape(lead + (2, 2, -1, array.shape[-1]))

    def with_gains(down, attn_scale, mlp_scale, lead, more=8):
        extra = jnp.stack([attn_scale.reshape(lead + (4, -1)), mlp_scale.reshape(lead + (4, -1))], axis=-2)
        pads = [(0, 0)] * (len(lead) + 1) + [(0, more - 2), (0, width - extra.shape[-1])]
        joined = jnp.concatenate(
            [down.astype(F32).reshape(lead + (4, -1, width)), jnp.pad(extra.astype(F32), pads)],
            axis=-2,
        )
        return quarters(joined.reshape(lead + (-1, width)).astype(BF16), lead)

    base = seq * rows
    ids = places - (base + jnp.arange(rows, dtype=jnp.int32))
    full_qkv, full_in, full_attn, full_down, ids_below, ids_above = gather_all(
        (quarters(w_qkv), quarters(w_in), quarters(w_attn),
         with_gains(w_down, gain_attn, gain_mlp, ())),
        ids.reshape(-1, 128), 0,
    )
    full_qkv = full_qkv.reshape(width, 3 * width)
    full_in = full_in.reshape(width, 2 * hidden)
    full_attn = full_attn.reshape(width, width)
    blocks_down = full_down.reshape(lines, 4, -1, width)
    full_down = blocks_down[:, :, :quarter_rows].reshape(hidden, width)
    gain_a = blocks_down[:, :, quarter_rows, : share // 4].reshape(1, width)
    gain_m = blocks_down[:, :, quarter_rows + 1, : share // 4].reshape(1, width)
    below = ids_below.reshape(-1)[rows - HALF :]
    above = ids_above.reshape(-1)[:HALF]
    nowhere = jnp.int32(-(1 << 30))
    below = jnp.where(seq == 0, nowhere, below)
    above = jnp.where(seq == seqs - 1, nowhere, above)
    ids_wide = jnp.concatenate([below, ids, above])
    blocks = rows // QROWS
    span = QROWS + 2 * HALF
    cols = jnp.stack([ids_wide[i * QROWS : i * QROWS + span] for i in range(blocks)])[:, None, :]

    lane = jnp.arange(PAIR, dtype=jnp.int32)
    quarter = HEAD_DIM // 2
    exponent = (lane % quarter).astype(F32) * (2.0 / HEAD_DIM)
    frequency = jnp.power(F32(10000.0), -exponent)
    angles = places.astype(F32)[:, None] * frequency[None, :]
    cosine = jnp.cos(angles)
    sine = jnp.where(lane % HEAD_DIM < quarter, -1.0, 1.0)[None, :] * jnp.sin(angles)

    big = rows // ROWS
    normed_attn, queries, kv = call(
        project_kernel, big, (x, gain_a, full_qkv, cosine, sine),
        [by_rows(ROWS, width), whole((1, width)), whole((width, 3 * width)),
         by_rows(ROWS, PAIR), by_rows(ROWS, PAIR)],
        [shape((rows, width), BF16), shape((rows, width), BF16), shape((rows, 2 * width), BF16)],
        [by_rows(ROWS, width), by_rows(ROWS, width), by_rows(ROWS, 2 * width)],
        6 * rows * width * width,
    )
    kv_below, kv_above = neighbours(kv[:HALF], kv[rows - HALF :])
    kv_wide = jnp.concatenate([kv_below, kv, kv_above], axis=0)
    pairs = width // PAIR
    probs_spec = pl.BlockSpec((1, pairs, 2 * QROWS, span), lambda i: (i, 0, 0, 0))
    attend_flops = 4 * blocks * pairs * 2 * QROWS * span * PAIR
    context, probs = call(
        attend_kernel, blocks, (queries, kv_wide, ids[:, None], cols),
        [by_rows(QROWS, width), whole((rows + 2 * HALF, 2 * width)), by_rows(QROWS, 1),
         pl.BlockSpec((1, 1, span), lambda i: (i, 0, 0))],
        [shape((rows, width), BF16), shape((blocks, pairs, 2 * QROWS, span), BF16)],
        [by_rows(QROWS, width), probs_spec],
        attend_flops,
    )
    mixed, normed_mlp, hidden_low, d_gate, d_resid, d_low, d_context, d_gain_m = call(
        mlp_kernel, big, (x, context, dy, gain_m, full_attn, full_in, full_down),
        [by_rows(ROWS, width), by_rows(ROWS, width), by_rows(ROWS, width), whole((1, width)),
         whole((width, width)), whole((width, 2 * hidden)), whole((hidden, width))],
        [shape((rows, width), BF16), shape((rows, width), BF16), shape((rows, hidden), BF16),
         shape((rows, 2 * hidden), BF16), shape((rows, width), F32), shape((rows, width), BF16),
         shape((rows, width), BF16), shape((1, width), F32)],
        [by_rows(ROWS, width), by_rows(ROWS, width), by_rows(ROWS, hidden),
         by_rows(ROWS, 2 * hidden), by_rows(ROWS, width), by_rows(ROWS, width),
         by_rows(ROWS, width), whole((1, width))],
        2 * rows * width * (2 * width + 6 * hidden),
    )

    def weight_grad(left, right):
        return lax.dot_general(left, right, FIRST, preferred_element_type=F32).astype(BF16)

    grad_in = weight_grad(normed_mlp, d_gate)
    grad_attn = weight_grad(context, d_low)
    grad_down = lax.dot_general(hidden_low, dy, FIRST, preferred_element_type=F32)

    lead = (lines,)
    (out_in, out_down, out_attn), (d_q, d_kv) = reduce_all(
        (quarters(grad_in, lead), with_gains(grad_down, d_gain_m[0], d_gain_m[0], lead),
         quarters(grad_attn, lead)),
        1, attend_back, (queries, kv_wide, probs, d_context, cosine, sine),
        (shape((rows, width), BF16), shape((rows + 2 * HALF, 2 * width), F32)),
    )
    from_below, from_above = neighbours(
        d_kv[:HALF].astype(BF16), d_kv[rows + HALF :].astype(BF16)
    )
    (d_qkv,) = call(
        finish_kernel, big, (d_q, d_kv, from_below, from_above, cosine, sine),
        [by_rows(ROWS, width), whole((rows + 2 * HALF, 2 * width)), whole((HALF, 2 * width)),
         whole((HALF, 2 * width)), by_rows(ROWS, PAIR), by_rows(ROWS, PAIR)],
        [shape((rows, 3 * width), BF16)],
        [by_rows(ROWS, 3 * width)],
        8 * rows * width,
    )
    grad_qkv = weight_grad(normed_attn, d_qkv)
    d_tokens, d_gain_a = call(
        norm_back_kernel, big, (x, gain_a, d_qkv, full_qkv, d_resid),
        [by_rows(ROWS, width), whole((1, width)), by_rows(ROWS, 3 * width),
         whole((width, 3 * width)), by_rows(ROWS, width)],
        [shape((rows, width), F32), shape((1, width), F32)],
        [by_rows(ROWS, width), whole((1, width))],
        6 * rows * width * width,
    )
    (out_qk, out_v), _ = reduce_all(
        (quarters(grad_qkv[:, : 2 * width], lead),
         with_gains(grad_qkv[:, 2 * width :], d_gain_a[0], d_gain_a[0], lead, 16)),
        2,
    )
    out_v = out_v.reshape(4, -1, width)
    rows_v = share // 4
    out_qkv = jnp.concatenate(
        [out_qk.reshape(share, 2 * width), out_v[:, :rows_v].reshape(share, width)], axis=1
    )
    out_down = out_down.reshape(4, -1, width)
    return (
        mixed[None],
        d_tokens[None],
        out_qkv.astype(F32),
        out_attn.reshape(share, width).astype(F32),
        out_in.reshape(share, 2 * hidden).astype(F32),
        out_down[:, :quarter_rows].reshape(-1, width).astype(F32),
        out_v[:, rows_v, : share // 4].reshape(-1).astype(F32),
        out_down[:, quarter_rows + 1, : share // 4].reshape(-1).astype(F32),
    )


def solution(mesh):
    rows = P("wsh", "seq", None)
    return jax.shard_map(
        body,
        mesh=mesh,
        in_specs=(
            rows, P("wsh", "seq"), P("wsh", None), P("wsh", None), P("wsh", None),
            P("wsh", None), P("wsh"), P("wsh"), rows,
        ),
        out_specs=(
            rows, rows, P("wsh", None), P("wsh", None), P("wsh", None), P("wsh", None),
            P("wsh"), P("wsh"),
        ),
        check_vma=False,
    )
```
